256 devices in a mesh: seq: 64 (over y_lo, z, x), ch: 4 (over y_hi, core).
Axes of the slice: x: 4, y: 4 (y_hi: 2, y_lo: 2; y = y_hi * 2 + y_lo), z: 8, core: 2. Of those that a mesh axis runs over, the one named last changes fastest.
Arguments:
- tokens: bfloat16 [2, 4096, 1536], P(None, 'seq', 'ch'), may hold values from -6 to 6
- norm_gain: bfloat16 [1536], replicated, may hold values from 0.5 to 2
- w_query: bfloat16 [1536, 512], P(None, 'ch'), may hold values from -1.5 to 1.5
- w_key: bfloat16 [1536, 512], P(None, 'ch'), may hold values from -0.15625 to 0.15625
- w_value: bfloat16 [1536, 1536], P(None, 'ch'), may hold values from -0.15625 to 0.15625
- w_out: bfloat16 [1536, 1536], P('ch'), may hold values from -0.15625 to 0.15625
- content_bias: bfloat16 [512], P('ch'), may hold values from -5 to 5
- rel_key: bfloat16 [32, 512], P(None, 'ch'), may hold values from -5 to 5
- rel_value: bfloat16 [32, 1536], P(None, 'ch'), may hold values from -5 to 5
- bucket_of: int32 [383], replicated, may hold values from 0 to 31, never falling along the last dimension, each value on 1 to 24 neighbouring positions
Outputs:
- mixed: bfloat16 [2, 4096, 1536], P(None, 'seq', 'ch')
The draws below stay inside these ranges and needn't reach their ends.
Inputs may be any that keep to these rules, and one draw needn't show every extreme that they name: `bucket_of`: never falls along its dimension; every bucket covers 1 to 24 consecutive distances, and one covers the most.
All inputs are finite; a program needn't handle non-finite values.
Results may differ from the reference program's by a relative error of at most 0.015.
The reference program's roundings to bfloat16 on the way count: a program that leaves them out, or rounds other values in their place, can miss the bound.
Values may be sent and summed in bfloat16 or wider, within the bound.
No kernel may reach another device: no remote copies, remote signals or barrier semaphores. Data moves between devices by JAX's collectives and lax.ppermute only.
A program may use at most 64 MiB of HBM per device.

```python
import math
import jax
import jax.numpy as jnp
import numpy as np
from jax import lax

D = 1536
HEADS = 8
KEY = 64
VAL = 192
NB = 32
REACH = 2
BLK = 64
SEQS = 2
LENGTH = 4096
DIST = 383
N_SEQ = 64
N_CH = 4


def draw_w_query(key, part):
    key = jax.random.fold_in(key, 11)
    return (jax.random.truncated_normal(key, -4.0, 4.0, (D, HEADS * KEY), jnp.float32) * D ** (-0.5)).astype(jnp.bfloat16)


def block_levels(key, dims, cuts, low, top_value):
    loudness = 1.0
    for axis_at, blocks in cuts:
        heights = jax.random.uniform(jax.random.fold_in(jax.random.fold_in(key, 6), axis_at), (blocks,), jnp.float32, low / len(cuts), top_value / len(cuts))
        loudness = loudness * jnp.repeat(jnp.exp(heights), dims[axis_at] // blocks).reshape((-1,) + (1,) * (len(dims) - 1 - axis_at))
    return loudness


def profile(count, total, most, skew):
    weights = [(1 << 20) // math.isqrt(rank ** skew) + 1 for rank in range(2, count + 1)]
    rest, given = total - most - (count - 1), [1] * (count - 1)
    while rest > 0:
        free = [i for i in range(count - 1) if given[i] < most]
        mass, budget = sum([weights[i] for i in free]), rest
        for i in free:
            extra = min(most - given[i], max(1, budget * weights[i] // mass), rest)
            given[i] = given[i] + extra
            rest = rest - extra
    return np.array([most] + given)


def ragged(key, number_of, total, most, slope):
    if number_of == 2:
        one = jax.random.randint(key, (), max(1, total - most), min(most, total - 1) + 1)
        return jnp.stack([one, total - one])
    sizes = jnp.asarray(profile(number_of, total, most, slope), jnp.int32)
    twos = (number_of - 1) // 2
    source_of, receiver = sizes[1:1 + 2 * twos:2], sizes[2:2 + 2 * twos:2]
    margin = jnp.minimum(source_of - 1, most - receiver)
    moved = jax.random.randint(jax.random.fold_in(key, 1), (twos,), 0, 1 << 20) % (margin + 1)
    sizes = sizes.at[1:1 + 2 * twos:2].set(source_of - moved).at[2:2 + 2 * twos:2].set(receiver + moved)
    return sizes[jax.random.permutation(jax.random.fold_in(key, 2), number_of)]


def centred(own_key, extent, scale, limit, shards=(), kind=jnp.bfloat16):
    result = jax.random.normal(own_key, extent, jnp.float32) * scale
    if len(shards) > 0:
        result = block_levels(own_key, extent, shards, -0.22, 0.18) * result
    return jnp.clip(result, min=-limit, max=limit).astype(kind)


def setup_inputs(seed: int = 0) -> dict:
    seeds = jax.random.split(jax.random.key(seed), 11)
    return {
        "tokens": centred(seeds[0], (SEQS, LENGTH, D), 1.0, 6.0, ((1, 64), (2, 4))),
        "norm_gain": jnp.clip(jnp.exp(jax.random.uniform(seeds[1], (D,), jnp.float32, math.log(0.5), math.log(2.0))), 0.5, 2.0).astype(jnp.bfloat16),
        "w_query": draw_w_query(jax.random.fold_in(seeds[10], 71), 0),
        "w_key": centred(seeds[3], (D, HEADS * KEY), D ** -0.5, 0.15625, ((1, 4),)),
        "w_value": centred(seeds[4], (D, HEADS * VAL), D ** -0.5, 0.15625, ((1, 4),)),
        "w_out": centred(seeds[5], (HEADS * VAL, D), (HEADS * VAL) ** -0.5, 0.15625, ((0, 4),)),
        "content_bias": centred(seeds[6], (HEADS * KEY,), 1.0, 5.0, ((0, 4),)),
        "rel_key": centred(seeds[7], (NB, HEADS * KEY), 1.0, 5.0, ((1, 4),)),
        "rel_value": centred(seeds[8], (NB, HEADS * VAL), 1.0, 5.0, ((1, 4),)),
        "bucket_of": jnp.searchsorted(jnp.cumsum(ragged(seeds[9], NB, DIST, (2 * REACH + 2) * BLK // 16, 0)), jnp.arange(DIST), side="right").astype(jnp.int32),
    }


eps = 1e-05

def normalize(rows, norm_gain):
    values = rows.astype(jnp.float32)
    center = lax.optimization_barrier(jnp.mean(values, axis=-1, keepdims=True))
    spread = lax.optimization_barrier(jnp.mean(jnp.square(values - center), axis=-1, keepdims=True))
    return ((values - center) * lax.rsqrt(spread + eps) * norm_gain.astype(jnp.float32)).astype(jnp.bfloat16)

def bucket_tables(bucket_of, block_rows, window_rows, buckets):
    distance = jnp.arange(window_rows, dtype=jnp.int32)[None, :] - jnp.arange(block_rows, dtype=jnp.int32)[:, None] + (block_rows - 1)
    index = jnp.take(bucket_of, distance).astype(jnp.int32)
    onehot = (index[:, :, None] == jnp.arange(buckets, dtype=jnp.int32)[None, None, :]).astype(jnp.bfloat16)
    return (index, onehot)

def attend(query, keys, values, content_bias, rel_key, rel_value, index, onehot):
    sequences, block_rows, _ = query.shape
    window_rows = keys.shape[1]
    heads = content_bias.shape[0] // KEY
    query_heads = query.astype(jnp.float32).reshape(sequences, block_rows, heads, KEY)
    key_heads = keys.astype(jnp.float32).reshape(sequences, window_rows, heads, KEY)
    value_heads = values.astype(jnp.float32).reshape(sequences, window_rows, heads, VAL)
    bias_heads = content_bias.astype(jnp.float32).reshape(heads, KEY)
    key_table = rel_key.astype(jnp.float32).reshape(-1, heads, KEY)
    value_table = rel_value.astype(jnp.float32).reshape(-1, heads, VAL)
    content = jnp.einsum('sihk,schk->shic', query_heads, key_heads)
    biased = jnp.einsum('schk,hk->shc', key_heads, bias_heads)
    by_bucket = jnp.einsum('sihk,bhk->shib', query_heads, key_table)
    picks = jnp.broadcast_to(index[None, None], (sequences, heads, block_rows, window_rows))
    position = jnp.take_along_axis(by_bucket, picks, axis=3)
    scores = (content + biased[:, :, None, :] + position) * KEY ** (-0.5)
    top = lax.optimization_barrier(jnp.max(scores, axis=-1, keepdims=True))
    expo = jnp.exp(scores - top)
    total = lax.optimization_barrier(jnp.sum(expo, axis=-1))
    weights = expo.astype(jnp.bfloat16).astype(jnp.float32)
    bucketed = jnp.einsum('shic,icb->shib', weights, onehot.astype(jnp.float32)).astype(jnp.bfloat16).astype(jnp.float32)
    summed = jnp.einsum('shic,schv->sihv', weights, value_heads) + jnp.einsum('shib,bhv->sihv', bucketed, value_table)
    context = summed / jnp.transpose(total, (0, 2, 1))[..., None]
    return context.astype(jnp.bfloat16).reshape(sequences, block_rows, heads * VAL)

def reference(tokens, norm_gain, w_query, w_key, w_value, w_out, content_bias, rel_key, rel_value, bucket_of):
    rows = SEQS * LENGTH
    normed = normalize(tokens, norm_gain).reshape(rows, D)
    query = jnp.dot(normed, w_query, preferred_element_type=jnp.float32).astype(jnp.bfloat16).reshape(SEQS, LENGTH, HEADS * KEY)
    keys = jnp.dot(normed, w_key, preferred_element_type=jnp.float32).astype(jnp.bfloat16).reshape(SEQS, LENGTH, HEADS * KEY)
    values = jnp.dot(normed, w_value, preferred_element_type=jnp.float32).astype(jnp.bfloat16).reshape(SEQS, LENGTH, HEADS * VAL)
    window_rows = (2 * REACH + 1) * BLK
    index, onehot = bucket_tables(bucket_of, BLK, window_rows, NB)
    group_width = HEADS // N_CH * VAL
    out_weight = w_out.astype(jnp.float32)

    def one_block(block):
        start = block * BLK
        query_block = lax.dynamic_slice_in_dim(query, start, BLK, 1)
        spots = (start - REACH * BLK + jnp.arange(window_rows, dtype=jnp.int32)) % LENGTH
        key_block = jnp.take(keys, spots, axis=1)
        value_block = jnp.take(values, spots, axis=1)
        context = attend(query_block, key_block, value_block, content_bias, rel_key, rel_value, index, onehot).astype(jnp.float32)
        summed = jnp.zeros((SEQS, BLK, D), jnp.float32)
        for group in range(N_CH):
            lower = group * group_width
            partial_value = jnp.einsum('sie,ed->sid', context[:, :, lower:lower + group_width], out_weight[lower:lower + group_width])
            summed = summed + lax.optimization_barrier(partial_value.astype(jnp.bfloat16)).astype(jnp.float32)
        residual = lax.dynamic_slice_in_dim(tokens, start, BLK, 1).astype(jnp.float32)
        return (residual + summed).astype(jnp.bfloat16)
    blocks = lax.map(one_block, jnp.arange(N_SEQ, dtype=jnp.int32))
    return jnp.transpose(blocks, (1, 0, 2, 3)).reshape(SEQS, LENGTH, D)
```

```python
import functools

import jax
import jax.numpy as jnp
from jax import lax
from jax.experimental import pallas as pl
from jax.experimental.pallas import tpu as pltpu
from jax.sharding import PartitionSpec as P

KEY = 64
VAL = 192
REACH = 2
BLK = 64
SPAN = 384
WINDOW = (2 * REACH + 1) * BLK
EPS = 1e-05
F32 = jnp.float32
BF16 = jnp.bfloat16

NT = (((1,), (1,)), ((), ()))
TN = (((0,), (0,)), ((), ()))
NN = (((1,), (0,)), ((), ()))


def dot(left, right, dims=NN):
    return lax.dot_general(left, right, dims, preferred_element_type=F32)


def by_head(rows):
    lane = lax.broadcasted_iota(jnp.int32, rows.shape, 1)
    zero = jnp.zeros_like(rows)
    return jnp.concatenate(
        [jnp.where(lane < KEY, rows, zero), jnp.where(lane >= KEY, rows, zero)], axis=0
    )


def one_hot(bucket_ref, buckets):
    return (
        bucket_ref[...] == lax.broadcasted_iota(jnp.int32, (buckets, bucket_ref.shape[1]), 0)
    ).astype(F32).astype(BF16)


def to_distance(weights):
    count = weights.shape[0]
    moved = jnp.concatenate(
        [
            pltpu.roll(weights[at : at + 8], BLK - 8 - at % BLK, 1) if at % BLK != BLK - 8 else weights[at : at + 8]
            for at in range(0, count, 8)
        ],
        axis=0,
    )
    rest = 7 - lax.broadcasted_iota(jnp.int32, moved.shape, 0) % 8
    for bit in (4, 2, 1):
        moved = jnp.where(rest & bit != 0, pltpu.roll(moved, bit, 1), moved)
    return moved


def project_kernel(whole_ref, gain_ref, key_ref, value_ref, normed_ref, packed_ref):
    sequences, rows, width = whole_ref.shape
    values = whole_ref[...].reshape(sequences * rows, width).astype(F32)
    center = jnp.mean(values, axis=-1, keepdims=True)
    moved = values - center
    spread = jnp.mean(jnp.square(moved), axis=-1, keepdims=True)
    normed = (moved * lax.rsqrt(spread + EPS) * gain_ref[...].astype(F32)).astype(BF16)
    normed_ref[...] = normed
    keys = dot(normed, key_ref[...]).astype(BF16)
    split = keys.shape[1]
    packed_ref[:, :, :split] = keys.reshape(sequences, rows, split)
    values_here = dot(normed, value_ref[...]).astype(BF16)
    packed_ref[:, :, split:] = values_here.reshape(sequences, rows, value_ref.shape[1])


def position_kernel(normed_ref, query_weight_ref, rel_key_ref, bucket_ref, query_ref, place_ref):
    query = dot(normed_ref[...], query_weight_ref[...]).astype(BF16)
    query_ref[...] = query
    hot = one_hot(bucket_ref, rel_key_ref.shape[0])
    by_distance = dot(rel_key_ref[...], hot, TN).astype(BF16)
    sequences = query.shape[0] // BLK
    for seq in range(sequences):
        stacked = by_head(query[seq * BLK : (seq + 1) * BLK])
        table = dot(stacked, by_distance)
        for head in range(2):
            part = table[head * BLK : (head + 1) * BLK]
            place_ref[seq, head * BLK : (head + 1) * BLK, :] = pltpu.roll(
                part, SPAN - (BLK - 1), 1, stride=1, stride_axis=0
            )


def attend_kernel(
    query_ref, place_ref, low2_ref, low1_ref, here_ref, up1_ref, up2_ref, bias_ref, rel_value_ref,
    bucket_ref, out_weight_ref, own_ref, first_ref, second_ref, third_ref,
):
    sequences = query_ref.shape[0] // BLK
    parts = (low2_ref, low1_ref, here_ref, up1_ref, up2_ref)
    wide = 2 * KEY
    hot = one_hot(bucket_ref, rel_value_ref.shape[0])
    bias = by_head(jnp.broadcast_to(bias_ref[...], (8, wide)))
    contexts = []
    for seq in range(sequences):
        stacked = by_head(query_ref[seq * BLK : (seq + 1) * BLK, :])
        keys = jnp.concatenate([part[seq, :, :wide] for part in parts], axis=0)
        values = jnp.concatenate([part[seq, :, wide:] for part in parts], axis=0)
        keys = jnp.concatenate([keys, jnp.zeros((SPAN - WINDOW, wide), BF16)], axis=0)
        values = jnp.concatenate([values, jnp.zeros((SPAN - WINDOW, 2 * VAL), BF16)], axis=0)
        content = dot(jnp.concatenate([stacked, bias], axis=0), keys, NT)
        biased = jnp.concatenate(
            [
                jnp.broadcast_to(content[2 * BLK : 2 * BLK + 1], (BLK, SPAN)),
                jnp.broadcast_to(content[2 * BLK + 8 : 2 * BLK + 9], (BLK, SPAN)),
            ],
            axis=0,
        )
        scores = (content[: 2 * BLK] + biased + place_ref[seq]) * KEY ** (-0.5)
        lane = lax.broadcasted_iota(jnp.int32, scores.shape, 1)
        scores = jnp.where(lane < WINDOW, scores, -jnp.inf)
        top = jnp.max(scores, axis=-1, keepdims=True)
        expo = jnp.exp(scores - top)
        total = jnp.sum(expo, axis=-1, keepdims=True)
        weights = expo.astype(BF16)
        rounded = weights.astype(F32)
        spread = to_distance(rounded).astype(BF16)
        bucketed = dot(spread, hot, NT).astype(BF16)
        summed = dot(weights, values) + dot(bucketed, rel_value_ref[...])
        summed = summed / total
        side = lax.broadcasted_iota(jnp.int32, (BLK, 2 * VAL), 1)
        contexts.append(jnp.where(side < VAL, summed[:BLK], summed[BLK:]).astype(BF16))
    context = jnp.concatenate(contexts, axis=0)
    me = lax.axis_index("ch")
    width = own_ref.shape[2]
    for order, target in enumerate((own_ref, first_ref, second_ref, third_ref)):
        at = pl.multiple_of((me ^ order) * width, width)
        partial_value = dot(context, out_weight_ref[:, pl.ds(at, width)]).astype(BF16)
        target[...] = partial_value.reshape(sequences, BLK, width)


def call(kernel, outs, cost):
    return pl.pallas_call(
        kernel,
        out_shape=outs,
        compiler_params=pltpu.CompilerParams(vmem_limit_bytes=16 * 1024 * 1024),
        cost_estimate=pl.CostEstimate(flops=cost, bytes_accessed=1 << 20, transcendentals=0),
    )


def shape(*dims, dtype=BF16):
    return jax.ShapeDtypeStruct(dims, dtype)


def shifted(value, axis, steps):
    count = lax.axis_size(axis)
    return lax.ppermute(value, axis, [(at, (at + steps) % count) for at in range(count)])


def crossed(value, axis, flip):
    count = lax.axis_size(axis)
    return lax.ppermute(value, axis, [(at, at ^ flip) for at in range(count)])


def body(
    tokens, norm_gain, w_query, w_key, w_value, w_out, content_bias, rel_key, rel_value, bucket_of
):
    sequences, rows, width = tokens.shape
    whole = lax.all_gather(tokens, "ch", axis=2, tiled=True)
    gain = norm_gain.reshape(1, -1)
    bias = content_bias.reshape(1, -1)
    bucket = jnp.pad(bucket_of, (0, SPAN - bucket_of.shape[0]), constant_values=-1).reshape(1, SPAN)
    packed_width = w_key.shape[1] + w_value.shape[1]
    normed, packed = call(
        project_kernel,
        [shape(sequences * rows, whole.shape[2]), shape(sequences, rows, packed_width)],
        300 << 20,
    )(whole, gain, w_key, w_value)
    up1 = shifted(packed, "seq", -1)
    low1 = shifted(packed, "seq", 1)
    up2 = shifted(packed, "seq", -2)
    low2 = shifted(packed, "seq", 2)
    query, place = call(
        position_kernel,
        [shape(sequences * rows, w_query.shape[1]), shape(sequences, 2 * BLK, SPAN, dtype=F32)],
        300 << 20,
    )(normed, w_query, rel_key, bucket)
    own, first, second, third = call(
        attend_kernel, [shape(sequences, rows, width)] * 4, 1 << 30
    )(query, place, low2, low1, packed, up1, up2, bias, rel_value, bucket, w_out)
    second = crossed(second, "ch", 2)
    third = crossed(third, "ch", 3)
    first = crossed(first, "ch", 1)
    summed = own.astype(F32) + first.astype(F32) + second.astype(F32) + third.astype(F32)
    return (tokens.astype(F32) + summed).astype(BF16)


def solution(mesh):
    return jax.shard_map(
        body,
        mesh=mesh,
        in_specs=(
            P(None, "seq", "ch"),
            P(),
            P(None, "ch"),
            P(None, "ch"),
            P(None, "ch"),
            P("ch", None),
            P("ch"),
            P(None, "ch"),
            P(None, "ch"),
            P(),
        ),
        out_specs=P(None, "seq", "ch"),
        check_vma=False,
    )
```

```python
import functools

import jax
import jax.numpy as jnp
from jax import lax
from jax.experimental import pallas as pl
from jax.experimental.pallas import tpu as pltpu
from jax.sharding import PartitionSpec as P

KEY = 64
VAL = 192
REACH = 2
BLK = 64
SPAN = 384
WINDOW = (2 * REACH + 1) * BLK
EPS = 1e-05
F32 = jnp.float32
BF16 = jnp.bfloat16

NT = (((1,), (1,)), ((), ()))
TN = (((0,), (0,)), ((), ()))
NN = (((1,), (0,)), ((), ()))


def dot(left, right, dims=NN):
    return lax.dot_general(left, right, dims, preferred_element_type=F32)


def by_head(rows):
    lane = lax.broadcasted_iota(jnp.int32, rows.shape, 1)
    zero = jnp.zeros_like(rows)
    return jnp.concatenate(
        [jnp.where(lane < KEY, rows, zero), jnp.where(lane >= KEY, rows, zero)], axis=0
    )


def one_hot(bucket_ref, buckets):
    return (
        bucket_ref[...] == lax.broadcasted_iota(jnp.int32, (buckets, bucket_ref.shape[1]), 0)
    ).astype(F32).astype(BF16)


def to_distance(weights):
    count = weights.shape[0]
    moved = jnp.concatenate(
        [
            pltpu.roll(weights[at : at + 8], BLK - 8 - at % BLK, 1) if at % BLK != BLK - 8 else weights[at : at + 8]
            for at in range(0, count, 8)
        ],
        axis=0,
    )
    rest = 7 - lax.broadcasted_iota(jnp.int32, moved.shape, 0) % 8
    for bit in (4, 2, 1):
        moved = jnp.where(rest & bit != 0, pltpu.roll(moved, bit, 1), moved)
    return moved


def project_kernel(
    own_ref, beside_ref, across_ref, corner_ref, gain_ref, key_ref, value_ref, query_weight_ref,
    packed_ref, query_ref,
):
    sequences, rows, width = own_ref.shape
    me = lax.axis_index("ch")
    pieces = [
        part[...].reshape(sequences * rows, width).astype(F32)
        for part in (own_ref, beside_ref, across_ref, corner_ref)
    ]
    count = len(pieces) * width
    center = sum(jnp.sum(piece, axis=-1, keepdims=True) for piece in pieces) / count
    pieces = [piece - center for piece in pieces]
    spread = sum(jnp.sum(jnp.square(piece), axis=-1, keepdims=True) for piece in pieces) / count
    scale = lax.rsqrt(spread + EPS)
    normed = []
    for order, piece in enumerate(pieces):
        at = pl.multiple_of((me ^ order) * width, width)
        gain = gain_ref[:, pl.ds(at, width)].astype(F32)
        normed.append((piece * scale * gain).astype(BF16))

    def project(weight_ref):
        return sum(
            dot(piece, weight_ref[pl.ds(pl.multiple_of((me ^ order) * width, width), width), :])
            for order, piece in enumerate(normed)
        ).astype(BF16)

    split = key_ref.shape[1]
    packed_ref[:, :, :split] = project(key_ref).reshape(sequences, rows, split)
    packed_ref[:, :, split:] = project(value_ref).reshape(sequences, rows, value_ref.shape[1])
    query_ref[...] = project(query_weight_ref)


def table_kernel(rel_key_ref, bucket_ref, gain_ref, table_ref, gain_out_ref):
    hot = one_hot(bucket_ref, rel_key_ref.shape[0])
    table_ref[...] = dot(rel_key_ref[...], hot, TN).astype(BF16)
    gain_out_ref[...] = gain_ref[...]


def position_kernel(query_ref, table_ref, place_ref):
    query = query_ref[...]
    sequences = query.shape[0] // BLK
    for seq in range(sequences):
        stacked = by_head(query[seq * BLK : (seq + 1) * BLK])
        table = dot(stacked, table_ref[...])
        for head in range(2):
            part = table[head * BLK : (head + 1) * BLK]
            place_ref[seq, head * BLK : (head + 1) * BLK, :] = pltpu.roll(
                part, SPAN - (BLK - 1), 1, stride=1, stride_axis=0
            )


def attend_kernel(
    query_ref, place_ref, up2_ref, up1_ref, here_ref, low1_ref, low2_ref, bias_ref, rel_value_ref,
    bucket_ref, out_weight_ref, own_ref, first_ref, second_ref, third_ref,
):
    sequences = query_ref.shape[0] // BLK
    parts = (low2_ref, low1_ref, here_ref, up1_ref, up2_ref)
    wide = 2 * KEY
    hot = one_hot(bucket_ref, rel_value_ref.shape[0])
    bias = by_head(jnp.broadcast_to(bias_ref[...], (8, wide)))
    contexts = []
    for seq in range(sequences):
        stacked = by_head(query_ref[seq * BLK : (seq + 1) * BLK, :])
        keys = jnp.concatenate([part[seq, :, :wide] for part in parts], axis=0)
        values = jnp.concatenate([part[seq, :, wide:] for part in parts], axis=0)
        keys = jnp.concatenate([keys, jnp.zeros((SPAN - WINDOW, wide), BF16)], axis=0)
        values = jnp.concatenate([values, jnp.zeros((SPAN - WINDOW, 2 * VAL), BF16)], axis=0)
        content = dot(jnp.concatenate([stacked, bias], axis=0), keys, NT)
        biased = jnp.concatenate(
            [
                jnp.broadcast_to(content[2 * BLK : 2 * BLK + 1], (BLK, SPAN)),
                jnp.broadcast_to(content[2 * BLK + 8 : 2 * BLK + 9], (BLK, SPAN)),
            ],
            axis=0,
        )
        scores = (content[: 2 * BLK] + biased + place_ref[seq]) * KEY ** (-0.5)
        lane = lax.broadcasted_iota(jnp.int32, scores.shape, 1)
        scores = jnp.where(lane < WINDOW, scores, -jnp.inf)
        top = jnp.max(scores, axis=-1, keepdims=True)
        expo = jnp.exp(scores - top)
        total = jnp.sum(expo, axis=-1, keepdims=True)
        weights = expo.astype(BF16)
        rounded = weights.astype(F32)
        spread = to_distance(rounded).astype(BF16)
        bucketed = dot(spread, hot, NT).astype(BF16)
        summed = dot(weights, values) + dot(bucketed, rel_value_ref[...])
        summed = summed / total
        side = lax.broadcasted_iota(jnp.int32, (BLK, 2 * VAL), 1)
        contexts.append(jnp.where(side < VAL, summed[:BLK], summed[BLK:]).astype(BF16))
    context = jnp.concatenate(contexts, axis=0)
    me = lax.axis_index("ch")
    width = own_ref.shape[2]
    for order, target in enumerate((own_ref, first_ref, second_ref, third_ref)):
        at = pl.multiple_of((me ^ order) * width, width)
        partial_value = dot(context, out_weight_ref[:, pl.ds(at, width)]).astype(BF16)
        target[...] = partial_value.reshape(sequences, BLK, width)


def call(kernel, outs, cost):
    return pl.pallas_call(
        kernel,
        out_shape=outs,
        compiler_params=pltpu.CompilerParams(vmem_limit_bytes=16 * 1024 * 1024),
        cost_estimate=pl.CostEstimate(flops=cost, bytes_accessed=1 << 20, transcendentals=0),
    )


def shape(*dims, dtype=BF16):
    return jax.ShapeDtypeStruct(dims, dtype)


def shifted(value, axis, steps):
    count = lax.axis_size(axis)
    return lax.ppermute(value, axis, [(at, (at + steps) % count) for at in range(count)])


def crossed(value, axis, flip):
    count = lax.axis_size(axis)
    return lax.ppermute(value, axis, [(at, at ^ flip) for at in range(count)])


def body(
    tokens, norm_gain, w_query, w_key, w_value, w_out, content_bias, rel_key, rel_value, bucket_of
):
    sequences, rows, width = tokens.shape
    gain = norm_gain.reshape(1, -1)
    bias = content_bias.reshape(1, -1)
    bucket = jnp.pad(bucket_of, (0, SPAN - bucket_of.shape[0]), constant_values=-1).reshape(1, SPAN)
    packed_width = w_key.shape[1] + w_value.shape[1]
    across = crossed(tokens, "ch", 2)
    beside = crossed(tokens, "ch", 1)
    table, gain = call(
        table_kernel, [shape(w_key.shape[1], SPAN), shape(*gain.shape)], 20 << 30
    )(rel_key, bucket, gain)
    across, table, gain = lax.optimization_barrier((across, table, gain))
    corner = crossed(across, "ch", 1)
    packed, query = call(
        project_kernel,
        [shape(sequences, rows, packed_width), shape(sequences * rows, w_query.shape[1])],
        300 << 20,
    )(tokens, beside, across, corner, gain, w_key, w_value, w_query)
    low2 = shifted(packed, "seq", 2)
    low1 = shifted(packed, "seq", 1)
    up1 = shifted(packed, "seq", -1)
    up2 = shifted(packed, "seq", -2)
    place = call(
        position_kernel, shape(sequences, 2 * BLK, SPAN, dtype=F32), 300 << 20
    )(query, table)
    own, beside, across, corner = call(
        attend_kernel, [shape(sequences, rows, width)] * 4, 1 << 30
    )(query, place, up2, up1, packed, low1, low2, bias, rel_value, bucket, w_out)
    pair = (across.astype(F32) + crossed(corner, "ch", 1).astype(F32)).astype(BF16)
    beside = crossed(beside, "ch", 1)
    pair = crossed(pair, "ch", 2)
    summed = own.astype(F32) + beside.astype(F32) + pair.astype(F32)
    return (tokens.astype(F32) + summed).astype(BF16)


def solution(mesh):
    return jax.shard_map(
        body,
        mesh=mesh,
        in_specs=(
            P(None, "seq", "ch"),
            P(),
            P(None, "ch"),
            P(None, "ch"),
            P(None, "ch"),
            P("ch", None),
            P("ch"),
            P(None, "ch"),
            P(None, "ch"),
            P(),
        ),
        out_specs=P(None, "seq", "ch"),
        check_vma=False,
    )
```

```python
import functools

import jax
import jax.numpy as jnp
from jax import lax
from jax.experimental import pallas as pl
from jax.experimental.pallas import tpu as pltpu
from jax.sharding import PartitionSpec as P

KEY = 64
VAL = 192
REACH = 2
BLK = 64
SPAN = 384
WINDOW = (2 * REACH + 1) * BLK
EPS = 1e-05
F32 = jnp.float32
BF16 = jnp.bfloat16

NT = (((1,), (1,)), ((), ()))
TN = (((0,), (0,)), ((), ()))
NN = (((1,), (0,)), ((), ()))


def dot(left, right, dims=NN):
    return lax.dot_general(left, right, dims, preferred_element_type=F32)


def by_head(rows):
    lane = lax.broadcasted_iota(jnp.int32, rows.shape, 1)
    zero = jnp.zeros_like(rows)
    return jnp.concatenate(
        [jnp.where(lane < KEY, rows, zero), jnp.where(lane >= KEY, rows, zero)], axis=0
    )


def one_hot(bucket_ref, buckets):
    return (
        bucket_ref[...] == lax.broadcasted_iota(jnp.int32, (buckets, bucket_ref.shape[1]), 0)
    ).astype(F32).astype(BF16)


def flip(rows):
    down = lax.broadcasted_iota(jnp.int32, (BLK, BLK), 0)
    along = lax.broadcasted_iota(jnp.int32, (BLK, BLK), 1)
    swap = (down + along == BLK - 1).astype(F32).astype(BF16)
    return dot(swap, rows).astype(BF16)


def to_window(table):
    count = table.shape[0]
    moved = jnp.concatenate(
        [
            pltpu.roll(table[at : at + 8], SPAN - at % BLK, 1) if at % BLK else table[at : at + 8]
            for at in range(0, count, 8)
        ],
        axis=0,
    )
    rest = lax.broadcasted_iota(jnp.int32, moved.shape, 0) % 8
    for bit in (4, 2, 1):
        moved = jnp.where(rest & bit != 0, pltpu.roll(moved, SPAN - bit, 1), moved)
    return moved


def project_kernel(
    own_ref, beside_ref, across_ref, corner_ref, gain_ref, key_ref, value_ref, query_weight_ref,
    packed_ref, query_ref,
):
    sequences, rows, width = own_ref.shape
    me = lax.axis_index("ch")
    pieces = [
        part[...].reshape(sequences * rows, width).astype(F32)
        for part in (own_ref, beside_ref, across_ref, corner_ref)
    ]
    count = len(pieces) * width
    center = sum(jnp.sum(piece, axis=-1, keepdims=True) for piece in pieces) / count
    pieces = [piece - center for piece in pieces]
    spread = sum(jnp.sum(jnp.square(piece), axis=-1, keepdims=True) for piece in pieces) / count
    scale = lax.rsqrt(spread + EPS)
    normed = []
    for order, piece in enumerate(pieces):
        at = pl.multiple_of((me ^ order) * width, width)
        gain = gain_ref[:, pl.ds(at, width)].astype(F32)
        normed.append((piece * scale * gain).astype(BF16))

    def project(weight_ref):
        return sum(
            dot(piece, weight_ref[pl.ds(pl.multiple_of((me ^ order) * width, width), width), :])
            for order, piece in enumerate(normed)
        ).astype(BF16)

    split = key_ref.shape[1]
    packed_ref[:, :, :split] = project(key_ref).reshape(sequences, rows, split)
    packed_ref[:, :, split:] = project(value_ref).reshape(sequences, rows, value_ref.shape[1])
    query_ref[...] = project(query_weight_ref)


def gain_kernel(gain_ref, gain_out_ref):
    gain_out_ref[...] = gain_ref[...]


def position_kernel(query_ref, rel_key_ref, bucket_ref, flipped_ref, place_ref):
    hot = one_hot(bucket_ref, rel_key_ref.shape[0])
    by_distance = dot(rel_key_ref[...], hot, TN).astype(BF16)
    for seq in range(place_ref.shape[0]):
        rows = slice(seq * BLK, (seq + 1) * BLK)
        flipped = flip(query_ref[rows, :])
        flipped_ref[rows, :] = flipped
        place_ref[seq] = to_window(dot(by_head(flipped), by_distance))


def attend_kernel(
    query_ref, place_ref, here_ref, up1_ref, up2_ref, low2_ref, low1_ref, bias_ref, rel_value_ref,
    bucket_ref, out_weight_ref, context_ref, corner_ref,
):
    sequences = query_ref.shape[0] // BLK
    parts = (low2_ref, low1_ref, here_ref, up1_ref, up2_ref)
    wide = 2 * KEY
    hot = one_hot(bucket_ref, rel_value_ref.shape[0])
    bias = by_head(jnp.broadcast_to(bias_ref[...], (8, wide)))
    contexts = []
    for seq in range(sequences):
        stacked = by_head(query_ref[seq * BLK : (seq + 1) * BLK, :])
        keys = jnp.concatenate([part[seq, :, :wide] for part in parts], axis=0)
        values = jnp.concatenate([part[seq, :, wide:] for part in parts], axis=0)
        keys = jnp.concatenate([keys, jnp.zeros((SPAN - WINDOW, wide), BF16)], axis=0)
        values = jnp.concatenate([values, jnp.zeros((SPAN - WINDOW, 2 * VAL), BF16)], axis=0)
        content = dot(jnp.concatenate([stacked, bias], axis=0), keys, NT)
        biased = jnp.concatenate(
            [
                jnp.broadcast_to(content[2 * BLK : 2 * BLK + 1], (BLK, SPAN)),
                jnp.broadcast_to(content[2 * BLK + 8 : 2 * BLK + 9], (BLK, SPAN)),
            ],
            axis=0,
        )
        scores = (content[: 2 * BLK] + biased + place_ref[seq]) * KEY ** (-0.5)
        lane = lax.broadcasted_iota(jnp.int32, scores.shape, 1)
        scores = jnp.where(lane < WINDOW, scores, -jnp.inf)
        top = jnp.max(scores, axis=-1, keepdims=True)
        expo = jnp.exp(scores - top)
        total = jnp.sum(expo, axis=-1, keepdims=True)
        weights = expo.astype(BF16)
        rounded = weights.astype(F32)
        spread = jnp.concatenate(
            [
                pltpu.roll(rounded[head * BLK : (head + 1) * BLK], 0, 1, stride=1, stride_axis=0)
                for head in range(2)
            ],
            axis=0,
        ).astype(BF16)
        bucketed = dot(spread, hot, NT).astype(BF16)
        summed = dot(weights, values) + dot(bucketed, rel_value_ref[...])
        summed = summed / total
        side = lax.broadcasted_iota(jnp.int32, (BLK, 2 * VAL), 1)
        contexts.append(flip(jnp.where(side < VAL, summed[:BLK], summed[BLK:]).astype(BF16)))
    context = jnp.concatenate(contexts, axis=0)
    context_ref[...] = context
    project_out(context, out_weight_ref, ((3, corner_ref),))


def project_out(context, out_weight_ref, targets):
    me = lax.axis_index("ch")
    for order, target in targets:
        sequences, rows, width = target.shape
        at = pl.multiple_of((me ^ order) * width, width)
        partial_value = dot(context, out_weight_ref[:, pl.ds(at, width)]).astype(BF16)
        target[...] = partial_value.reshape(sequences, rows, width)


def output_kernel(context_ref, out_weight_ref, own_ref, beside_ref, across_ref):
    project_out(
        context_ref[...], out_weight_ref, ((2, across_ref), (1, beside_ref), (0, own_ref))
    )


def call(kernel, outs, cost):
    return pl.pallas_call(
        kernel,
        out_shape=outs,
        compiler_params=pltpu.CompilerParams(vmem_limit_bytes=16 * 1024 * 1024),
        cost_estimate=pl.CostEstimate(flops=cost, bytes_accessed=1 << 20, transcendentals=0),
    )


def shape(*dims, dtype=BF16):
    return jax.ShapeDtypeStruct(dims, dtype)


def shifted(value, axis, steps):
    count = lax.axis_size(axis)
    return lax.ppermute(value, axis, [(at, (at + steps) % count) for at in range(count)])


def crossed(value, axis, flip):
    count = lax.axis_size(axis)
    return lax.ppermute(value, axis, [(at, at ^ flip) for at in range(count)])


def body(
    tokens, norm_gain, w_query, w_key, w_value, w_out, content_bias, rel_key, rel_value, bucket_of
):
    sequences, rows, width = tokens.shape
    gain = norm_gain.reshape(1, -1)
    bias = content_bias.reshape(1, -1)
    bucket = jnp.pad(bucket_of, (0, SPAN - bucket_of.shape[0]), constant_values=-1).reshape(1, SPAN)
    packed_width = w_key.shape[1] + w_value.shape[1]
    across = crossed(tokens, "ch", 2)
    gain = call(gain_kernel, shape(*gain.shape), 20 << 30)(gain)
    beside, gain = lax.optimization_barrier((tokens, gain))
    beside = crossed(beside, "ch", 1)
    across, gain = lax.optimization_barrier((across, gain))
    corner = crossed(across, "ch", 1)
    packed, query = call(
        project_kernel,
        [shape(sequences, rows, packed_width), shape(sequences * rows, w_query.shape[1])],
        300 << 20,
    )(tokens, beside, across, corner, gain, w_key, w_value, w_query)
    low2 = shifted(packed, "seq", 2)
    low1 = shifted(packed, "seq", 1)
    up1 = shifted(packed, "seq", -1)
    up2 = shifted(packed, "seq", -2)
    flipped, place = call(
        position_kernel, [shape(*query.shape), shape(sequences, 2 * BLK, SPAN, dtype=F32)], 300 << 20
    )(query, rel_key, bucket)
    context, corner = call(
        attend_kernel, [shape(sequences * rows, w_out.shape[0]), shape(sequences, rows, width)], 1 << 30
    )(flipped, place, packed, up1, up2, low2, low1, bias, rel_value, bucket, w_out)
    own, beside, across = call(output_kernel, [shape(sequences, rows, width)] * 3, 300 << 20)(
        context, w_out
    )
    pair = (across.astype(F32) + crossed(corner, "ch", 1).astype(F32)).astype(BF16)
    beside = crossed(beside, "ch", 1)
    pair = crossed(pair, "ch", 2)
    summed = own.astype(F32) + beside.astype(F32) + pair.astype(F32)
    return (tokens.astype(F32) + summed).astype(BF16)


def solution(mesh):
    return jax.shard_map(
        body,
        mesh=mesh,
        in_specs=(
            P(None, "seq", "ch"),
            P(),
            P(None, "ch"),
            P(None, "ch"),
            P(None, "ch"),
            P("ch", None),
            P("ch"),
            P(None, "ch"),
            P(None, "ch"),
            P(),
        ),
        out_specs=P(None, "seq", "ch"),
        check_vma=False,
    )
```
